32 devices in a mesh: groups: 2 (over y), tensor: 8 (over z, x), dp: 2 (over core).
Axes of the slice: x: 2, y: 2, z: 4, core: 2. Of those that a mesh axis runs over, the one named last changes fastest.
Arguments:
- activations: bfloat16 [8192, 64, 512], P('tensor', ('groups', 'dp')), parts along dimension 1, may hold values from -6 to 6
- out_grads: bfloat16 [8192, 64, 512], P('tensor', ('groups', 'dp')), parts along dimension 1, may hold values from -6 to 6
- proj_in: bfloat16 [8192, 64], P('tensor'), may hold values from -0.0625 to 0.0625
- proj_out: bfloat16 [8192, 64], P('tensor'), may hold values from -0.0625 to 0.0625
- padding: int32 [64], P(('groups', 'dp')), parts along dimension 0, may hold values from 0 to 255
- queries: float32 [512, 4096], P(('groups', 'dp')), parts along dimension 0, may hold values from -6 to 6
Outputs:
- scores: float32 [64, 256], P(('groups', 'dp')), parts along dimension 0
The draws below stay inside these ranges and needn't reach their ends.
There are 2 independent parts, one for each index of `groups`. The reference program is written for one: setup_inputs(seed, part) draws one part's arguments, and reference() takes and returns one part's arrays. A program takes and returns all parts, laid end to end along the dimension named above; an argument that names none is the same for every part. Nothing has to cross between parts.
All inputs are finite; a program needn't handle non-finite values.
Results may differ from the reference program's by a relative error of at most 0.0003.
Values may be sent and summed in bfloat16 or wider, within the bound.
A program may use at most 128 MiB of HBM per device.

```python
import jax
import jax.numpy as jnp
from jax import lax

D = 8192
R = 64
SEQ = 512
NQ = 256
EXAMPLES = 32


def plant(entries, rng, smallest, top_value):
    longest = entries.shape.index(max(entries.shape))
    spots = []
    for shift in (0, 1):
        where = [jax.random.randint(jax.random.fold_in(rng, axis), (), 0, length) for axis, length in enumerate(entries.shape)]
        where[longest] = (where[longest] + shift) % entries.shape[longest]
        spots.append(tuple(where))
    return entries.at[spots[0]].set(smallest).at[spots[1]].set(top_value)


def levels(own_key, extent, pieces, low, top_value):
    level, own = 1.0, jax.random.fold_in(own_key, 6)
    for dim, shards_of in pieces:
        draws = jnp.exp(jax.random.uniform(jax.random.fold_in(own, dim), (shards_of,), jnp.float32, low / len(pieces), top_value / len(pieces)))
        level = level * jnp.repeat(draws, extent[dim] // shards_of).reshape([-1 if axis == dim else 1 for axis in range(len(extent))])
    return level


def gaussian(rng, dims, spread, reach, split=(), held_as=jnp.bfloat16):
    result = spread * jax.random.normal(rng, dims, jnp.float32)
    if split:
        result = result * levels(rng, dims, split, -0.22, 0.18)
    return jnp.clip(result, -reach, reach).astype(held_as)


def setup_inputs(seed: int = 0, part: int = 0) -> dict:
    keys = jax.random.split(jax.random.key(seed), 7)
    part_keys = jax.random.split(jax.random.fold_in(keys[6], part), 7)
    activations = gaussian(part_keys[0], (D, EXAMPLES, SEQ), 1.0, 6.0, ((0, 8), (1, 2)))
    out_grads = gaussian(part_keys[1], (D, EXAMPLES, SEQ), 1.0, 6.0, ((0, 8), (1, 2)))
    proj_in = gaussian(keys[2], (D, R), D ** -0.5, 0.0625, ((0, 8),))
    proj_out = gaussian(keys[3], (D, R), D ** -0.5, 0.0625, ((0, 8),))
    padding = plant(jax.random.randint(part_keys[4], (EXAMPLES,), 0, SEQ // 2), jax.random.fold_in(part_keys[4], 1), 0, (SEQ // 2) - 1).astype(jnp.int32)
    queries = gaussian(part_keys[5], (NQ, R * R), 1.0, 6.0, ((0, 2),), jnp.float32)
    return {"activations": activations, "out_grads": out_grads, "proj_in": proj_in, "proj_out": proj_out, "padding": padding, "queries": queries}


def reference(activations, out_grads, proj_in, proj_out, padding, queries):
    highest = lax.Precision.HIGHEST
    act_proj = jnp.einsum("dr,des->res", proj_in.astype(jnp.float32), activations.astype(jnp.float32), precision=highest)
    grad_proj = jnp.einsum("dr,des->res", proj_out.astype(jnp.float32), out_grads.astype(jnp.float32), precision=highest)
    slots = jnp.arange(SEQ, dtype=jnp.int32)
    limit = (SEQ - padding).astype(jnp.int32)
    live = (slots[None, :] < limit[:, None]).astype(jnp.float32)
    count = limit.astype(jnp.float32)
    masked = grad_proj * live[None, :, :]
    summed = jnp.einsum("aes,bes->eab", masked, act_proj, precision=highest)
    example_grads = (summed / count[:, None, None]).reshape(EXAMPLES, R * R)
    return jnp.dot(example_grads, queries.T, precision=highest, preferred_element_type=jnp.float32)
```

```python
import functools

import jax
import jax.numpy as jnp
from jax import lax
from jax.experimental import pallas as pl
from jax.experimental.pallas import tpu as pltpu
from jax.sharding import PartitionSpec as P

MESH = pl.DeviceIdType.MESH
LEVELS = 32767.0


def quantize(values, data_ref, scale_ref, row):
    top = jnp.maximum(jnp.max(jnp.abs(values), axis=0, keepdims=True), 1e-30)
    data_ref[...] = jnp.round(values * (LEVELS / top)).astype(jnp.int32).astype(jnp.int16)
    step = top * (1.0 / LEVELS)
    tiles = values.shape[1] // 128
    for tile in range(tiles):
        scale_ref[pl.ds(row * tiles + tile, 1), :] = step[:, tile * 128 : (tile + 1) * 128]


def restore(data_ref, scale_ref, row):
    tiles = data_ref.shape[1] // 128
    step = jnp.concatenate([scale_ref[pl.ds(row * tiles + tile, 1), :] for tile in range(tiles)], axis=1)
    return data_ref[...].astype(jnp.int32).astype(jnp.float32) * step


def halves(values):
    high = values.astype(jnp.bfloat16)
    return high, (values - high.astype(jnp.float32)).astype(jnp.bfloat16)


def reduce_and_score(
    n, act_ref, grad_ref, padding_ref, queries_ref, out_ref,
    xs, xs_scale, xr, xr_scale, zs, zs_scale, zr, zr_scale, total, all_queries, query_high, query_low, rows, results,
    xd_sem, xf_sem, zd_sem, zf_sem, q_sem, out_send, out_recv,
):
    examples, rank, seq = act_ref.shape
    own = examples // n
    steps = n // 2
    me, core = lax.axis_index("tensor"), lax.axis_index("dp")
    z, x = me // 2, lax.rem(me, 2)
    parts = (act_ref, grad_ref)

    barrier = pltpu.get_barrier_semaphore()
    for shift in range(1, n):
        pl.semaphore_signal(barrier, inc=1, device_id={"tensor": lax.rem(me + shift, n)}, device_id_type=MESH)
    pl.semaphore_signal(barrier, inc=1, device_id={"dp": 1 - core}, device_id_type=MESH)
    pl.semaphore_wait(barrier, n)

    def send(source, target, send_sem, recv_sem, device):
        return pltpu.make_async_remote_copy(
            src_ref=source, dst_ref=target, send_sem=send_sem, recv_sem=recv_sem, device_id=device, device_id_type=MESH
        )

    def x_copies(c):
        device = {"tensor": z * 2 + (1 - x)}
        return (
            send(xs.at[c], xr.at[c], xd_sem.at[0, c], xd_sem.at[1, c], device),
            send(xs_scale.at[c], xr_scale.at[c], xf_sem.at[0, c], xf_sem.at[1, c], device),
        )

    def z_copies(c):
        goal = lax.rem(z + (steps - 1 - c // own), steps)
        device = {"tensor": goal * 2 + x}
        return (
            send(zs.at[c], zr.at[c], zd_sem.at[0, c], zd_sem.at[1, c], device),
            send(zs_scale.at[c], zr_scale.at[c], zf_sem.at[0, c], zf_sem.at[1, c], device),
        )

    def example(c, parity):
        goal = lax.rem(z + (steps - 1 - c // own), steps)
        return (goal * 2 + parity) * own + lax.rem(c, own)

    def first(c, carry):
        e = example(c, 1 - x)
        for k in range(2):
            quantize(parts[k][e], xs.at[c, k], xs_scale.at[c], k)
        for copy in x_copies(c):
            copy.start()
        return carry

    lax.fori_loop(0, steps * own, first, 0)

    local = pltpu.make_async_copy(queries_ref, all_queries.at[core], q_sem.at[2])
    other = send(queries_ref, all_queries.at[core], q_sem.at[0], q_sem.at[1], {"dp": 1 - core})
    local.start()
    other.start()

    def second(c, carry):
        for copy in x_copies(c):
            copy.wait_recv()
        e = example(c, x)
        for k in range(2):
            quantize(parts[k][e] + restore(xr.at[c, k], xr_scale.at[c], k), zs.at[c, k], zs_scale.at[c], k)
        for copy in z_copies(c):
            copy.start()
        return carry

    sent = (steps - 1) * own
    lax.fori_loop(0, sent, second, 0)

    local.wait()
    other.wait()
    count = queries_ref.shape[0]
    for half in range(2):
        high, low = halves(all_queries[half])
        query_high[half * count : (half + 1) * count] = high
        query_low[half * count : (half + 1) * count] = low

    for i in range(own):
        c = sent + i
        for copy in x_copies(c):
            copy.wait_recv()
        e = example(c, x)
        for k in range(2):
            total[i, k] = parts[k][e] + restore(xr.at[c, k], xr_scale.at[c], k)

    def third(c, carry):
        for copy in z_copies(c):
            copy.wait_recv()
        i = lax.rem(c, own)
        for k in range(2):
            total[i, k] = total[i, k] + restore(zr.at[c, k], zr_scale.at[c], k)
        return carry

    lax.fori_loop(0, sent, third, 0)

    slots = lax.broadcasted_iota(jnp.int32, (1, seq), 1)
    rows[...] = jnp.zeros_like(rows)
    for i in range(own):
        limit = seq - padding_ref[0, me * own + i]
        live = slots < limit
        act = jnp.concatenate(halves(total[i, 0]), axis=0)
        grad = jnp.concatenate(halves(jnp.where(live, total[i, 1], 0.0)), axis=0)
        summed = lax.dot_general(grad, act, (((1,), (1,)), ((), ())), preferred_element_type=jnp.float32)
        summed = summed[:rank, :rank] + summed[:rank, rank:] + summed[rank:, :rank]
        summed = summed / jnp.full((1, 1), limit, jnp.int32).astype(jnp.float32)
        for a in range(rank):
            rows[i : i + 1, a * rank : (a + 1) * rank] = summed[a : a + 1, :]
    row_high, row_low = halves(rows[...])
    stacked = jnp.concatenate([row_high.astype(jnp.float32), row_low.astype(jnp.float32)], axis=0).astype(jnp.bfloat16)
    contract = (((1,), (1,)), ((), ()))
    by_high = lax.dot_general(stacked, query_high[...], contract, preferred_element_type=jnp.float32)
    by_low = lax.dot_general(stacked, query_low[...], contract, preferred_element_type=jnp.float32)
    results[me] = by_high[:8] + by_high[8:] + by_low[:8]

    def result_copy(shift):
        return send(
            results.at[me], results.at[me], out_send.at[shift - 1], out_recv.at[shift - 1],
            {"tensor": lax.rem(me + shift, n)},
        )

    for shift in range(1, n):
        result_copy(shift).start()
    for shift in range(1, n):
        source = lax.rem(me + (n - shift), n)
        send(
            results.at[source], results.at[source], out_send.at[shift - 1], out_recv.at[shift - 1],
            {"tensor": lax.rem(me + shift, n)},
        ).wait_recv()
    for t in range(n):
        out_ref[t * own : (t + 1) * own, :] = results[t][:own]
    for shift in range(1, n):
        result_copy(shift).wait_send()

    def sent_x(c, carry):
        for copy in x_copies(c):
            copy.wait_send()
        return carry

    def sent_z(c, carry):
        for copy in z_copies(c):
            copy.wait_send()
        return carry

    lax.fori_loop(0, steps * own, sent_x, 0)
    lax.fori_loop(0, sent, sent_z, 0)


def fused(n, act_part, grad_part, padding, queries):
    examples, rank, seq = act_part.shape
    own = examples // n
    x_chunks, z_chunks = examples // 2, examples // 2 - own
    scale_rows = 2 * seq // 128
    count, width = queries.shape
    vmem = pl.BlockSpec(memory_space=pltpu.VMEM)
    return pl.pallas_call(
        functools.partial(reduce_and_score, n),
        out_shape=jax.ShapeDtypeStruct((examples, 2 * count), jnp.float32),
        in_specs=[vmem, vmem, pl.BlockSpec(memory_space=pltpu.SMEM), pl.BlockSpec(memory_space=pl.ANY)],
        out_specs=vmem,
        scratch_shapes=[
            pltpu.VMEM((x_chunks, 2, rank, seq), jnp.int16),
            pltpu.VMEM((x_chunks, scale_rows, 128), jnp.float32),
            pltpu.VMEM((x_chunks, 2, rank, seq), jnp.int16),
            pltpu.VMEM((x_chunks, scale_rows, 128), jnp.float32),
            pltpu.VMEM((z_chunks, 2, rank, seq), jnp.int16),
            pltpu.VMEM((z_chunks, scale_rows, 128), jnp.float32),
            pltpu.VMEM((z_chunks, 2, rank, seq), jnp.int16),
            pltpu.VMEM((z_chunks, scale_rows, 128), jnp.float32),
            pltpu.VMEM((own, 2, rank, seq), jnp.float32),
            pltpu.VMEM((2, count, width), jnp.float32),
            pltpu.VMEM((2 * count, width), jnp.bfloat16),
            pltpu.VMEM((2 * count, width), jnp.bfloat16),
            pltpu.VMEM((8, width), jnp.float32),
            pltpu.VMEM((n, 8, 2 * count), jnp.float32),
            pltpu.SemaphoreType.DMA((2, x_chunks)),
            pltpu.SemaphoreType.DMA((2, x_chunks)),
            pltpu.SemaphoreType.DMA((2, z_chunks)),
            pltpu.SemaphoreType.DMA((2, z_chunks)),
            pltpu.SemaphoreType.DMA((3,)),
            pltpu.SemaphoreType.DMA((n - 1,)),
            pltpu.SemaphoreType.DMA((n - 1,)),
        ],
        compiler_params=pltpu.CompilerParams(
            collective_id=0, has_side_effects=True, vmem_limit_bytes=40 << 20
        ),
    )(act_part, grad_part, padding.reshape(1, examples), queries)


def plain(act_part, grad_part, padding, queries):
    act_proj, grad_proj = lax.psum((act_part, grad_part), "tensor")
    examples, rank, seq = act_proj.shape
    limit = seq - padding
    live = (jnp.arange(seq, dtype=jnp.int32)[None, :] < limit[:, None]).astype(jnp.float32)
    summed = jnp.einsum("eas,ebs->eab", grad_proj * live[:, None, :], act_proj, precision=lax.Precision.HIGHEST)
    grad_rows = (summed / limit.astype(jnp.float32)[:, None, None]).reshape(examples, rank * rank)
    gathered = lax.all_gather(queries, "dp", axis=0, tiled=True)
    return jnp.dot(grad_rows, gathered.T, precision=lax.Precision.HIGHEST, preferred_element_type=jnp.float32)


def per_device(n, cores, activations, out_grads, proj_in, proj_out, padding, queries):
    act_part = jnp.einsum("dr,des->ers", proj_in, activations, preferred_element_type=jnp.float32)
    grad_part = jnp.einsum("dr,des->ers", proj_out, out_grads, preferred_element_type=jnp.float32)
    examples = activations.shape[1]
    if cores == 2 and n % 2 == 0 and n >= 4 and examples % n == 0 and examples // n <= 8:
        return fused(n, act_part, grad_part, padding, queries)
    return plain(act_part, grad_part, padding, queries)


def solution(mesh):
    placed = (
        P("tensor", ("groups", "dp"), None),
        P("tensor", ("groups", "dp"), None),
        P("tensor", None),
        P("tensor", None),
        P(("groups", "dp")),
        P(("groups", "dp"), None),
    )
    return jax.shard_map(
        functools.partial(per_device, mesh.shape["tensor"], mesh.shape["dp"]),
        mesh=mesh, in_specs=placed, out_specs=P(("groups", "dp"), None), check_vma=False,
    )
```

```python
import functools

import jax
import jax.numpy as jnp
from jax import lax
from jax.experimental import pallas as pl
from jax.experimental.pallas import tpu as pltpu
from jax.sharding import PartitionSpec as P

MESH = pl.DeviceIdType.MESH
LEVELS = 32767.0


LANES = 128


def quantize(values, data_ref, scale_ref, row):
    top = jnp.maximum(jnp.max(jnp.abs(values), axis=0, keepdims=True), 1e-30)
    data_ref[...] = jnp.round(values * (LEVELS / top)).astype(jnp.int32).astype(jnp.int16)
    scale_ref[row : row + 1, :] = top * (1.0 / LEVELS)


def restore(data_ref, scale_ref, row):
    return data_ref[...].astype(jnp.int32).astype(jnp.float32) * scale_ref[row : row + 1, :]


def halves(values):
    high = values.astype(jnp.bfloat16)
    return high, (values - high.astype(jnp.float32)).astype(jnp.bfloat16)


def example_major(block, turned):
    for d in range(0, block.shape[0], 16):
        rows = jnp.swapaxes(block[d : d + 16], 0, 1)
        for e in range(16):
            turned[e // 2, d : d + 16, (e % 2) * LANES : (e % 2 + 1) * LANES] = rows[e]


def project(weights, turned, part):
    for pair in range(turned.shape[0]):
        both = lax.dot_general(
            weights[...], turned[pair], (((1,), (0,)), ((), ())), preferred_element_type=jnp.float32
        )
        part[2 * pair] = both[:, :LANES]
        part[2 * pair + 1] = both[:, LANES:]


def attribute(
    n, act_ref, grad_ref, proj_in_ref, proj_out_ref, padding_ref, queries_ref, out_ref,
    act_block, grad_block, act_turned, grad_turned, weights, part,
    xs, xs_scale, xr, xr_scale, zs, zs_scale, zr, zr_scale, total, all_queries, query_high, query_low, rows, results,
    in_sem, xd_sem, xf_sem, zd_sem, zf_sem, q_sem, out_send, out_recv,
):
    examples, seq = act_ref.shape[1:]
    rank = proj_in_ref.shape[1]
    own = examples // n
    steps = n // 2
    tiles = seq // LANES
    me, core = lax.axis_index("tensor"), lax.axis_index("dp")
    z, x = me // 2, lax.rem(me, 2)

    def fetch(source, block, tile, sem):
        lanes = pl.ds(pl.multiple_of(tile * LANES, LANES), LANES)
        return pltpu.make_async_copy(source.at[:, :, lanes], block, in_sem.at[sem])

    fetch(act_ref, act_block, 0, 0).start()
    fetch(grad_ref, grad_block, 0, 1).start()

    barrier = pltpu.get_barrier_semaphore()
    for shift in range(1, n):
        pl.semaphore_signal(barrier, inc=1, device_id={"tensor": lax.rem(me + shift, n)}, device_id_type=MESH)
    pl.semaphore_signal(barrier, inc=1, device_id={"dp": 1 - core}, device_id_type=MESH)

    weights[0] = proj_in_ref[...].astype(jnp.float32).T.astype(jnp.bfloat16)
    weights[1] = proj_out_ref[...].astype(jnp.float32).T.astype(jnp.bfloat16)

    def send(source, target, send_sem, recv_sem, device):
        return pltpu.make_async_remote_copy(
            src_ref=source, dst_ref=target, send_sem=send_sem, recv_sem=recv_sem, device_id=device, device_id_type=MESH
        )

    def owner(j):
        return lax.rem(z + (steps - 1 - j), steps)

    def x_copies(tile, j):
        device = {"tensor": z * 2 + (1 - x)}
        return (
            send(xs.at[tile, j], xr.at[tile, j], xd_sem.at[0, tile, j], xd_sem.at[1, tile, j], device),
            send(xs_scale.at[tile, j], xr_scale.at[tile, j], xf_sem.at[0, tile, j], xf_sem.at[1, tile, j], device),
        )

    def z_copies(tile, j):
        device = {"tensor": owner(j) * 2 + x}
        return (
            send(zs.at[tile, j], zr.at[tile, j], zd_sem.at[0, tile, j], zd_sem.at[1, tile, j], device),
            send(zs_scale.at[tile, j], zr_scale.at[tile, j], zf_sem.at[0, tile, j], zf_sem.at[1, tile, j], device),
        )

    pairs = [(i, k) for i in range(own) for k in range(2)]

    def to_x(tile):
        def one(j, carry):
            base = (owner(j) * 2 + (1 - x)) * own
            for i, k in pairs:
                quantize(part[tile, k, base + i], xs.at[tile, j, i, k], xs_scale.at[tile, j], 2 * i + k)
            for copy in x_copies(tile, j):
                copy.start()
            return carry

        lax.fori_loop(0, steps, one, 0)

    def x_to_z(tile):
        def one(j, carry):
            for copy in x_copies(tile, j):
                copy.wait_recv()
            base = (owner(j) * 2 + x) * own
            for i, k in pairs:
                arrived = restore(xr.at[tile, j, i, k], xr_scale.at[tile, j], 2 * i + k)
                quantize(part[tile, k, base + i] + arrived, zs.at[tile, j, i, k], zs_scale.at[tile, j], 2 * i + k)
            for copy in z_copies(tile, j):
                copy.start()
            return carry

        lax.fori_loop(0, steps - 1, one, 0)

    def local_queries():
        return pltpu.make_async_copy(queries_ref, all_queries.at[core], q_sem.at[2])

    def other_queries():
        return send(queries_ref, all_queries.at[core], q_sem.at[0], q_sem.at[1], {"dp": 1 - core})

    def project_tile(tile, carry):
        fetch(act_ref, act_block, tile, 0).wait()
        example_major(act_block, act_turned)

        @pl.when(tile < tiles - 1)
        def _():
            fetch(act_ref, act_block, tile + 1, 0).start()

        fetch(grad_ref, grad_block, tile, 1).wait()
        example_major(grad_block, grad_turned)
        project(weights.at[0], act_turned, part.at[tile, 0])

        @pl.when(tile < tiles - 1)
        def _():
            fetch(grad_ref, grad_block, tile + 1, 1).start()

        project(weights.at[1], grad_turned, part.at[tile, 1])

        @pl.when(tile == 0)
        def _():
            pl.semaphore_wait(barrier, n)

        to_x(tile)

        @pl.when(tile == 0)
        def _():
            local_queries().start()
            other_queries().start()

        @pl.when(tile > 0)
        def _():
            x_to_z(tile - 1)

        return carry

    lax.fori_loop(0, tiles, project_tile, 0)

    local_queries().wait()
    other_queries().wait()
    count = queries_ref.shape[0]
    for half in range(2):
        high, low = halves(all_queries[half])
        query_high[half * count : (half + 1) * count] = high
        query_low[half * count : (half + 1) * count] = low

    x_to_z(tiles - 1)

    def finish(tile, carry):
        for copy in x_copies(tile, steps - 1):
            copy.wait_recv()
        base = (z * 2 + x) * own
        sums = [
            part[tile, k, base + i] + restore(xr.at[tile, steps - 1, i, k], xr_scale.at[tile, steps - 1], 2 * i + k)
            for i, k in pairs
        ]
        for j in range(steps - 1):
            for copy in z_copies(tile, j):
                copy.wait_recv()
            sums = [
                s + restore(zr.at[tile, j, i, k], zr_scale.at[tile, j], 2 * i + k) for s, (i, k) in zip(sums, pairs)
            ]
        for s, (i, k) in zip(sums, pairs):
            total[tile, i, k] = s
        return carry

    lax.fori_loop(0, tiles, finish, 0)

    slots = lax.broadcasted_iota(jnp.int32, (1, seq), 1)
    rows[...] = jnp.zeros_like(rows)
    contract = (((1,), (1,)), ((), ()))
    for i in range(own):
        limit = seq - padding_ref[0, me * own + i]
        act = jnp.concatenate([total[tile, i, 0] for tile in range(tiles)], axis=1)
        grad = jnp.concatenate([total[tile, i, 1] for tile in range(tiles)], axis=1)
        act = jnp.concatenate(halves(act), axis=0)
        grad = jnp.concatenate(halves(jnp.where(slots < limit, grad, 0.0)), axis=0)
        summed = lax.dot_general(grad, act, contract, preferred_element_type=jnp.float32)
        summed = summed[:rank, :rank] + summed[:rank, rank:] + summed[rank:, :rank]
        summed = summed / jnp.full((1, 1), limit, jnp.int32).astype(jnp.float32)
        for a in range(rank):
            rows[i : i + 1, a * rank : (a + 1) * rank] = summed[a : a + 1, :]
    row_high, row_low = halves(rows[...])
    stacked = jnp.concatenate([row_high.astype(jnp.float32), row_low.astype(jnp.float32)], axis=0).astype(jnp.bfloat16)
    by_high = lax.dot_general(stacked, query_high[...], contract, preferred_element_type=jnp.float32)
    by_low = lax.dot_general(stacked, query_low[...], contract, preferred_element_type=jnp.float32)
    results[me] = by_high[:8] + by_high[8:] + by_low[:8]

    def result_copy(shift, slot):
        return send(
            results.at[slot], results.at[slot], out_send.at[shift - 1], out_recv.at[shift - 1],
            {"tensor": lax.rem(me + shift, n)},
        )

    for shift in range(1, n):
        result_copy(shift, me).start()

    def sent(tile, carry):
        for j in range(steps):
            for copy in x_copies(tile, j):
                copy.wait_send()
        for j in range(steps - 1):
            for copy in z_copies(tile, j):
                copy.wait_send()
        return carry

    lax.fori_loop(0, tiles, sent, 0)
    for shift in range(1, n):
        result_copy(shift, lax.rem(me + (n - shift), n)).wait_recv()
    for t in range(n):
        out_ref[t * own : (t + 1) * own, :] = results[t][:own]
    for shift in range(1, n):
        result_copy(shift, me).wait_send()


def fused(n, activations, out_grads, proj_in, proj_out, padding, queries):
    features, examples, seq = activations.shape
    rank = proj_in.shape[1]
    own, steps, tiles = examples // n, n // 2, seq // LANES
    count, width = queries.shape
    vmem, hbm = pl.BlockSpec(memory_space=pltpu.VMEM), pl.BlockSpec(memory_space=pl.ANY)

    def crossing(chunks):
        return [
            pltpu.VMEM((tiles, chunks, own, 2, rank, LANES), jnp.int16),
            pltpu.VMEM((tiles, chunks, 8, LANES), jnp.float32),
        ] * 2

    return pl.pallas_call(
        functools.partial(attribute, n),
        out_shape=jax.ShapeDtypeStruct((examples, 2 * count), jnp.float32),
        in_specs=[hbm, hbm, vmem, vmem, pl.BlockSpec(memory_space=pltpu.SMEM), hbm],
        out_specs=vmem,
        scratch_shapes=[
            pltpu.VMEM((features, examples, LANES), jnp.bfloat16),
            pltpu.VMEM((features, examples, LANES), jnp.bfloat16),
            pltpu.VMEM((examples // 2, features, 2 * LANES), jnp.bfloat16),
            pltpu.VMEM((examples // 2, features, 2 * LANES), jnp.bfloat16),
            pltpu.VMEM((2, rank, features), jnp.bfloat16),
            pltpu.VMEM((tiles, 2, examples, rank, LANES), jnp.float32),
            *crossing(steps),
            *crossing(steps - 1),
            pltpu.VMEM((tiles, own, 2, rank, LANES), jnp.float32),
            pltpu.VMEM((2, count, width), jnp.float32),
            pltpu.VMEM((2 * count, width), jnp.bfloat16),
            pltpu.VMEM((2 * count, width), jnp.bfloat16),
            pltpu.VMEM((8, width), jnp.float32),
            pltpu.VMEM((n, 8, 2 * count), jnp.float32),
            pltpu.SemaphoreType.DMA((2,)),
            pltpu.SemaphoreType.DMA((2, tiles, steps)),
            pltpu.SemaphoreType.DMA((2, tiles, steps)),
            pltpu.SemaphoreType.DMA((2, tiles, steps - 1)),
            pltpu.SemaphoreType.DMA((2, tiles, steps - 1)),
            pltpu.SemaphoreType.DMA((3,)),
            pltpu.SemaphoreType.DMA((n - 1,)),
            pltpu.SemaphoreType.DMA((n - 1,)),
        ],
        compiler_params=pltpu.CompilerParams(
            collective_id=0, has_side_effects=True, vmem_limit_bytes=48 << 20
        ),
    )(activations, out_grads, proj_in, proj_out, padding.reshape(1, examples), queries)


def plain(act_part, grad_part, padding, queries):
    act_proj, grad_proj = lax.psum((act_part, grad_part), "tensor")
    examples, rank, seq = act_proj.shape
    limit = seq - padding
    live = (jnp.arange(seq, dtype=jnp.int32)[None, :] < limit[:, None]).astype(jnp.float32)
    summed = jnp.einsum("eas,ebs->eab", grad_proj * live[:, None, :], act_proj, precision=lax.Precision.HIGHEST)
    grad_rows = (summed / limit.astype(jnp.float32)[:, None, None]).reshape(examples, rank * rank)
    gathered = lax.all_gather(queries, "dp", axis=0, tiled=True)
    return jnp.dot(grad_rows, gathered.T, precision=lax.Precision.HIGHEST, preferred_element_type=jnp.float32)


def per_device(n, cores, activations, out_grads, proj_in, proj_out, padding, queries):
    features, examples, seq = activations.shape
    whole_tiles = examples == 16 and features % 16 == 0 and seq % LANES == 0
    if cores == 2 and n % 2 == 0 and n >= 4 and examples % n == 0 and examples // n <= 4 and whole_tiles:
        return fused(n, activations, out_grads, proj_in, proj_out, padding, queries)
    act_part = jnp.einsum("dr,des->ers", proj_in, activations, preferred_element_type=jnp.float32)
    grad_part = jnp.einsum("dr,des->ers", proj_out, out_grads, preferred_element_type=jnp.float32)
    return plain(act_part, grad_part, padding, queries)


def solution(mesh):
    placed = (
        P("tensor", ("groups", "dp"), None),
        P("tensor", ("groups", "dp"), None),
        P("tensor", None),
        P("tensor", None),
        P(("groups", "dp")),
        P(("groups", "dp"), None),
    )
    return jax.shard_map(
        functools.partial(per_device, mesh.shape["tensor"], mesh.shape["dp"]),
        mesh=mesh, in_specs=placed, out_specs=P(("groups", "dp"), None), check_vma=False,
    )
```

```python
import functools
import math

import jax
import jax.numpy as jnp
from jax import lax
from jax.experimental import pallas as pl
from jax.experimental.pallas import tpu as pltpu
from jax.sharding import PartitionSpec as P

MESH = pl.DeviceIdType.MESH
LEVELS = 32767.0


LANES = 128


def quantize(values, data_ref, scale_ref, row):
    top = jnp.maximum(jnp.max(jnp.abs(values), axis=0, keepdims=True), 1e-30)
    data_ref[...] = jnp.round(values * (LEVELS / top)).astype(jnp.int32).astype(jnp.int16)
    scale_ref[row : row + 1, :] = top * (1.0 / LEVELS)


def restore(data_ref, scale_ref, row):
    return data_ref[...].astype(jnp.int32).astype(jnp.float32) * scale_ref[row : row + 1, :]


def halves(values):
    high = values.astype(jnp.bfloat16)
    return high, (values - high.astype(jnp.float32)).astype(jnp.bfloat16)


def example_major(block, turned):
    for d in range(0, block.shape[0], 16):
        rows = jnp.swapaxes(block[d : d + 16], 0, 1)
        for e in range(16):
            turned[e // 2, d : d + 16, (e % 2) * LANES : (e % 2 + 1) * LANES] = rows[e]


def project(weights, turned, part):
    for pair in range(turned.shape[0]):
        both = lax.dot_general(
            weights[...], turned[pair], (((1,), (0,)), ((), ())), preferred_element_type=jnp.float32
        )
        part[2 * pair] = both[:, :LANES]
        part[2 * pair + 1] = both[:, LANES:]


def attribute(
    n, act_ref, grad_ref, proj_in_ref, proj_out_ref, padding_ref, queries_ref, out_ref,
    act_block, grad_block, act_turned, grad_turned, weights, part,
    xs, xs_scale, xr, xr_scale, zs, zs_scale, zr, zr_scale, total, all_queries, query_high, query_low, rows, results,
    in_sem, xd_sem, xf_sem, zd_sem, zf_sem, q_sem, out_send, out_recv,
):
    examples, seq = act_ref.shape[1:]
    rank = proj_in_ref.shape[0]
    own = examples // n
    steps = n // 2
    tiles = seq // LANES
    me, core = lax.axis_index("tensor"), lax.axis_index("dp")
    z, x = me // 2, lax.rem(me, 2)

    def fetch(source, block, tile, sem):
        lanes = pl.ds(pl.multiple_of(tile * LANES, LANES), LANES)
        return pltpu.make_async_copy(source.at[:, :, lanes], block, in_sem.at[sem])

    fetch(act_ref, act_block, 0, 0).start()
    fetch(grad_ref, grad_block, 0, 1).start()
    factors = [
        pltpu.make_async_copy(ref, weights.at[k], in_sem.at[2 + k]) for k, ref in enumerate((proj_in_ref, proj_out_ref))
    ]
    for copy in factors:
        copy.start()

    barrier = pltpu.get_barrier_semaphore()
    for shift in range(1, n):
        pl.semaphore_signal(barrier, inc=1, device_id={"tensor": lax.rem(me + shift, n)}, device_id_type=MESH)
    pl.semaphore_signal(barrier, inc=1, device_id={"dp": 1 - core}, device_id_type=MESH)

    for copy in factors:
        copy.wait()

    def send(source, target, send_sem, recv_sem, device):
        return pltpu.make_async_remote_copy(
            src_ref=source, dst_ref=target, send_sem=send_sem, recv_sem=recv_sem, device_id=device, device_id_type=MESH
        )

    def owner(j):
        return lax.rem(z + (steps - 1 - j), steps)

    def x_copies(tile, k, j):
        device, at = {"tensor": z * 2 + (1 - x)}, (tile, k, j)
        return (
            send(xs.at[at], xr.at[at], xd_sem.at[0, *at], xd_sem.at[1, *at], device),
            send(xs_scale.at[at], xr_scale.at[at], xf_sem.at[0, *at], xf_sem.at[1, *at], device),
        )

    def z_copies(tile, j):
        device = {"tensor": owner(j) * 2 + x}
        return (
            send(zs.at[tile, j], zr.at[tile, j], zd_sem.at[0, tile, j], zd_sem.at[1, tile, j], device),
            send(zs_scale.at[tile, j], zr_scale.at[tile, j], zf_sem.at[0, tile, j], zf_sem.at[1, tile, j], device),
        )

    pairs = [(i, k) for i in range(own) for k in range(2)]

    def to_x(tile, k):
        def one(j, carry):
            base = (owner(j) * 2 + (1 - x)) * own
            for i in range(own):
                quantize(part[tile, k, base + i], xs.at[tile, k, j, i], xs_scale.at[tile, k, j], i)
            for copy in x_copies(tile, k, j):
                copy.start()
            return carry

        lax.fori_loop(0, steps, one, 0)

    def x_to_z(tile):
        def one(j, carry):
            for copy in (*x_copies(tile, 0, j), *x_copies(tile, 1, j)):
                copy.wait_recv()
            base = (owner(j) * 2 + x) * own
            for i, k in pairs:
                arrived = restore(xr.at[tile, k, j, i], xr_scale.at[tile, k, j], i)
                quantize(part[tile, k, base + i] + arrived, zs.at[tile, j, i, k], zs_scale.at[tile, j], 2 * i + k)
            for copy in z_copies(tile, j):
                copy.start()
            return carry

        lax.fori_loop(0, steps - 1, one, 0)

    def local_queries():
        return pltpu.make_async_copy(queries_ref, all_queries.at[core], q_sem.at[2])

    def other_queries():
        return send(queries_ref, all_queries.at[core], q_sem.at[0], q_sem.at[1], {"dp": 1 - core})

    def project_tile(tile, carry):
        fetch(act_ref, act_block, tile, 0).wait()
        example_major(act_block, act_turned)

        @pl.when(tile < tiles - 1)
        def _():
            fetch(act_ref, act_block, tile + 1, 0).start()

        project(weights.at[0], act_turned, part.at[tile, 0])

        to_x(tile, 0)

        fetch(grad_ref, grad_block, tile, 1).wait()
        example_major(grad_block, grad_turned)

        @pl.when(tile < tiles - 1)
        def _():
            fetch(grad_ref, grad_block, tile + 1, 1).start()

        project(weights.at[1], grad_turned, part.at[tile, 1])

        to_x(tile, 1)

        @pl.when(tile > 0)
        def _():
            x_to_z(tile - 1)

        return carry

    pl.semaphore_wait(barrier, n)
    other_queries().start()
    local_queries().start()
    lax.fori_loop(0, tiles, project_tile, 0)

    local_queries().wait()
    other_queries().wait()
    count = queries_ref.shape[0]
    for half in range(2):
        high, low = halves(all_queries[half])
        query_high[half * count : (half + 1) * count] = high
        query_low[half * count : (half + 1) * count] = low

    x_to_z(tiles - 1)

    def finish(tile, carry):
        for copy in (*x_copies(tile, 0, steps - 1), *x_copies(tile, 1, steps - 1)):
            copy.wait_recv()
        base = (z * 2 + x) * own
        sums = [
            part[tile, k, base + i] + restore(xr.at[tile, k, steps - 1, i], xr_scale.at[tile, k, steps - 1], i)
            for i, k in pairs
        ]
        for j in range(steps - 1):
            for copy in z_copies(tile, j):
                copy.wait_recv()
            sums = [
                s + restore(zr.at[tile, j, i, k], zr_scale.at[tile, j], 2 * i + k) for s, (i, k) in zip(sums, pairs)
            ]
        for s, (i, k) in zip(sums, pairs):
            total[tile, i, k] = s
        return carry

    lax.fori_loop(0, tiles, finish, 0)

    slots = lax.broadcasted_iota(jnp.int32, (1, seq), 1)
    rows[...] = jnp.zeros_like(rows)
    contract = (((1,), (1,)), ((), ()))
    for i in range(own):
        limit = seq - padding_ref[0, me * own + i]
        act = jnp.concatenate([total[tile, i, 0] for tile in range(tiles)], axis=1)
        grad = jnp.concatenate([total[tile, i, 1] for tile in range(tiles)], axis=1)
        act = jnp.concatenate(halves(act), axis=0)
        grad = jnp.concatenate(halves(jnp.where(slots < limit, grad, 0.0)), axis=0)
        summed = lax.dot_general(grad, act, contract, preferred_element_type=jnp.float32)
        summed = summed[:rank, :rank] + summed[:rank, rank:] + summed[rank:, :rank]
        summed = summed / jnp.full((1, 1), limit, jnp.int32).astype(jnp.float32)
        for a in range(rank):
            rows[i : i + 1, a * rank : (a + 1) * rank] = summed[a : a + 1, :]
    row_high, row_low = halves(rows[...])
    stacked = jnp.concatenate([row_high.astype(jnp.float32), row_low.astype(jnp.float32)], axis=0).astype(jnp.bfloat16)
    by_high = lax.dot_general(stacked, query_high[...], contract, preferred_element_type=jnp.float32)
    by_low = lax.dot_general(stacked, query_low[...], contract, preferred_element_type=jnp.float32)
    results[me] = by_high[:8] + by_high[8:] + by_low[:8]

    def result_copy(shift, slot):
        return send(
            results.at[slot], results.at[slot], out_send.at[shift - 1], out_recv.at[shift - 1],
            {"tensor": lax.rem(me + shift, n)},
        )

    for shift in range(1, n):
        result_copy(shift, me).start()

    def sent(tile, carry):
        for j in range(steps):
            for copy in (*x_copies(tile, 0, j), *x_copies(tile, 1, j)):
                copy.wait_send()
        for j in range(steps - 1):
            for copy in z_copies(tile, j):
                copy.wait_send()
        return carry

    lax.fori_loop(0, tiles, sent, 0)
    for shift in range(1, n):
        result_copy(shift, lax.rem(me + (n - shift), n)).wait_recv()
    for t in range(n):
        out_ref[t * own : (t + 1) * own, :] = results[t][:own]
    for shift in range(1, n):
        result_copy(shift, me).wait_send()


def fused(n, activations, out_grads, proj_in, proj_out, padding, queries):
    features, examples, seq = activations.shape
    rank = proj_in.shape[1]
    own, steps, tiles = examples // n, n // 2, seq // LANES
    count, width = queries.shape
    vmem, hbm = pl.BlockSpec(memory_space=pltpu.VMEM), pl.BlockSpec(memory_space=pl.ANY)

    def crossing(lead, blocks):
        return [
            pltpu.VMEM((*lead, *blocks, rank, LANES), jnp.int16),
            pltpu.VMEM((*lead, math.prod(blocks), LANES), jnp.float32),
        ] * 2

    return pl.pallas_call(
        functools.partial(attribute, n),
        out_shape=jax.ShapeDtypeStruct((examples, 2 * count), jnp.float32),
        in_specs=[hbm, hbm, hbm, hbm, pl.BlockSpec(memory_space=pltpu.SMEM), hbm],
        out_specs=vmem,
        scratch_shapes=[
            pltpu.VMEM((features, examples, LANES), jnp.bfloat16),
            pltpu.VMEM((features, examples, LANES), jnp.bfloat16),
            pltpu.VMEM((examples // 2, features, 2 * LANES), jnp.bfloat16),
            pltpu.VMEM((examples // 2, features, 2 * LANES), jnp.bfloat16),
            pltpu.VMEM((2, rank, features), jnp.bfloat16),
            pltpu.VMEM((tiles, 2, examples, rank, LANES), jnp.float32),
            *crossing((tiles, 2, steps), (own,)),
            *crossing((tiles, steps - 1), (own, 2)),
            pltpu.VMEM((tiles, own, 2, rank, LANES), jnp.float32),
            pltpu.VMEM((2, count, width), jnp.float32),
            pltpu.VMEM((2 * count, width), jnp.bfloat16),
            pltpu.VMEM((2 * count, width), jnp.bfloat16),
            pltpu.VMEM((8, width), jnp.float32),
            pltpu.VMEM((n, 8, 2 * count), jnp.float32),
            pltpu.SemaphoreType.DMA((4,)),
            pltpu.SemaphoreType.DMA((2, tiles, 2, steps)),
            pltpu.SemaphoreType.DMA((2, tiles, 2, steps)),
            pltpu.SemaphoreType.DMA((2, tiles, steps - 1)),
            pltpu.SemaphoreType.DMA((2, tiles, steps - 1)),
            pltpu.SemaphoreType.DMA((3,)),
            pltpu.SemaphoreType.DMA((n - 1,)),
            pltpu.SemaphoreType.DMA((n - 1,)),
        ],
        compiler_params=pltpu.CompilerParams(
            collective_id=0, has_side_effects=True, vmem_limit_bytes=48 << 20
        ),
    )(activations, out_grads, proj_in.T, proj_out.T, padding.reshape(1, examples), queries)


def plain(act_part, grad_part, padding, queries):
    act_proj, grad_proj = lax.psum((act_part, grad_part), "tensor")
    examples, rank, seq = act_proj.shape
    limit = seq - padding
    live = (jnp.arange(seq, dtype=jnp.int32)[None, :] < limit[:, None]).astype(jnp.float32)
    summed = jnp.einsum("eas,ebs->eab", grad_proj * live[:, None, :], act_proj, precision=lax.Precision.HIGHEST)
    grad_rows = (summed / limit.astype(jnp.float32)[:, None, None]).reshape(examples, rank * rank)
    gathered = lax.all_gather(queries, "dp", axis=0, tiled=True)
    return jnp.dot(grad_rows, gathered.T, precision=lax.Precision.HIGHEST, preferred_element_type=jnp.float32)


def per_device(n, cores, activations, out_grads, proj_in, proj_out, padding, queries):
    features, examples, seq = activations.shape
    whole_tiles = examples == 16 and features % 16 == 0 and seq % LANES == 0
    if cores == 2 and n % 2 == 0 and n >= 4 and examples % n == 0 and examples // n <= 4 and whole_tiles:
        return fused(n, activations, out_grads, proj_in, proj_out, padding, queries)
    act_part = jnp.einsum("dr,des->ers", proj_in, activations, preferred_element_type=jnp.float32)
    grad_part = jnp.einsum("dr,des->ers", proj_out, out_grads, preferred_element_type=jnp.float32)
    return plain(act_part, grad_part, padding, queries)


def solution(mesh):
    placed = (
        P("tensor", ("groups", "dp"), None),
        P("tensor", ("groups", "dp"), None),
        P("tensor", None),
        P("tensor", None),
        P(("groups", "dp")),
        P(("groups", "dp"), None),
    )
    return jax.shard_map(
        functools.partial(per_device, mesh.shape["tensor"], mesh.shape["dp"]),
        mesh=mesh, in_specs=placed, out_specs=P(("groups", "dp"), None), check_vma=False,
    )
```
